768 devices in a mesh: dp: 96 (over y, z), mp: 8 (over x, core).
Axes of the slice: x: 4, y: 8, z: 12, core: 2. Of those that a mesh axis runs over, the one named last changes fastest.
Arguments:
- hidden_acts: bfloat16 [30720, 15360], P('dp', 'mp'), may hold values from -20 to 20
- out_grad: bfloat16 [30720, 6144], P('dp'), may hold values from -6 to 6
- basis: bfloat16 [6144, 512], replicated, may hold values from -0.078125 to 0.078125
- code_first: int32 [15360, 512], P(('mp', 'dp')), may hold values from -127 to 127
- scale_first: float32 [15360, 2], P(('mp', 'dp')), may hold values from 0.05 to 0.3
- code_second: int32 [15360, 512], P(('mp', 'dp')), may hold values from 16 to 255
- scale_second: float32 [15360, 2], P(('mp', 'dp')), may hold values from 0.0005 to 0.004
Outputs:
- weight_update: bfloat16 [15360, 6144], P('mp', 'dp')
- first_new: float32 [15360, 512], P(('mp', 'dp'))
- second_new: float32 [15360, 512], P(('mp', 'dp'))
The draws below stay inside these ranges and needn't reach their ends.
All inputs are finite; a program needn't handle non-finite values.
Results may differ from the reference program's by a relative error of at most 0.011.
Values may be sent and summed in bfloat16 or wider, within the bound.
A program may use at most 64 MiB of HBM per device.

```python
import math
import jax
import jax.numpy as jnp
from jax import lax

D_WIN = 6144
FF_WIN = 15360
RANK = 512
QBLOCK = 256
TOKENS = 30720


def place_ends(values, rng, least, largest):
    index_at = [jax.random.randint(jax.random.fold_in(rng, axis), (), 0, length) for axis, length in enumerate(values.shape)]
    longest = values.shape.index(max(values.shape))
    beside = index_at[:longest] + [(index_at[longest] + 1) % values.shape[longest]] + index_at[longest + 1:]
    return values.at[tuple(index_at)].set(least).at[tuple(beside)].set(largest)


def strengthened(entries, key, source, target, parts, factor):
    def block_of(axis_at):
        return (jnp.arange(entries.shape[axis_at]) // (entries.shape[axis_at] // parts)).reshape((-1,) + (1,) * (entries.ndim - 1 - axis_at))

    one_side = jax.random.permutation(key, parts)[block_of(target)]
    far = (block_of(target) + parts // 2) % parts
    return jnp.where((block_of(source) == one_side) | (block_of(source) == far), factor * entries, entries)


def level_of(key, shape, cuts, smallest, largest):
    loudness, own = 1.0, jax.random.fold_in(key, 6)
    for position, blocks in cuts:
        heights = jnp.exp(jax.random.uniform(jax.random.fold_in(own, position), (blocks,), jnp.float32, smallest / len(cuts), largest / len(cuts)))
        loudness = loudness * jnp.repeat(heights, shape[position] // blocks).reshape([-1 if axis == position else 1 for axis in range(len(shape))])
    return loudness


def bell_draw(stream_key, dims, deviation, limit, shards=(), kind=jnp.bfloat16):
    level = level_of(stream_key, dims, shards, -0.22, 0.18) if shards else 1.0
    result = jax.random.normal(stream_key, dims, jnp.float32) * deviation * level
    return jnp.minimum(jnp.maximum(result, -limit), limit).astype(kind)


def bell_draw_with(own_key, dims, spread, limit, shards, heavy, held_as=jnp.bfloat16):
    drawn = spread * jax.random.normal(own_key, dims, jnp.float32)
    if shards:
        drawn = drawn * level_of(own_key, dims, shards, -0.22, 0.18)
    return jnp.clip(strengthened(drawn, jax.random.fold_in(own_key, 3), *heavy), -limit, limit).astype(held_as)


def setup_inputs(seed: int = 0) -> dict:
    key_of = jax.random.split(jax.random.key(seed), 8)
    hidden_acts = bell_draw_with(key_of[0], (TOKENS, FF_WIN), 1.0, 20.0, ((0, 96), (1, 8)), (0, 1, 96, 4.75))
    out_grad = bell_draw(key_of[1], (TOKENS, D_WIN), 1.0, 6.0, ((0, 96),))
    basis = bell_draw(key_of[2], (D_WIN, RANK), D_WIN ** -0.5, 0.078125)
    code_first = place_ends(jax.random.randint(key_of[3], (FF_WIN, RANK), -127, 128), jax.random.fold_in(key_of[3], 1), -127, 127).astype(jnp.int32)
    scale_first = jnp.clip(jnp.exp(math.log(0.3) - 1.7917595 * jax.random.uniform(key_of[4], (FF_WIN, RANK // QBLOCK), jnp.float32) ** level_of(key_of[4], (FF_WIN, RANK // QBLOCK), ((0, 768),), -0.2, 0.2)), 0.05, 0.3)
    code_second = place_ends(jax.random.randint(key_of[5], (FF_WIN, RANK), 16, 256), jax.random.fold_in(key_of[5], 1), 16, 255).astype(jnp.int32)
    scale_second = jnp.clip(jnp.exp(math.log(0.004) - 2.0794415 * jax.random.uniform(key_of[6], (FF_WIN, RANK // QBLOCK), jnp.float32) ** level_of(key_of[6], (FF_WIN, RANK // QBLOCK), ((0, 768),), -0.2, 0.2)), 0.0005, 0.004)
    return {"hidden_acts": hidden_acts, "out_grad": out_grad, "basis": basis, "code_first": code_first, "scale_first": scale_first, "code_second": code_second, "scale_second": scale_second}


def dequant(codes, scales, block_len):
    row_count = codes.shape[0]
    shaped = codes.astype(jnp.float32).reshape(row_count, scales.shape[1], block_len)
    return (shaped, scales[:, :, None])

def reference(hidden_acts, out_grad, basis, code_first, scale_first, code_second, scale_second):
    factor = jnp.dot(out_grad, basis, preferred_element_type=jnp.float32).astype(jnp.bfloat16)
    projected = lax.dot_general(hidden_acts, factor, (((0,), (0,)), ((), ())), preferred_element_type=jnp.float32)
    low_grad = projected / math.sqrt(TOKENS)
    shaped_first, block_first = dequant(code_first, scale_first, QBLOCK)
    first_old = (shaped_first / 127.0 * block_first).reshape(code_first.shape)
    shaped_second, block_second = dequant(code_second, scale_second, QBLOCK)
    second_old = ((shaped_second / 255.0) ** 2 * block_second).reshape(code_second.shape)
    first_new = 0.9 * first_old + 0.1 * low_grad
    second_new = 0.999 * second_old + 0.001 * low_grad * low_grad
    normalized = (first_new / 0.19 / (jnp.sqrt(second_new / 0.001999) + 1e-08)).astype(jnp.bfloat16)
    weight_update = lax.dot_general(normalized, basis, (((1,), (1,)), ((), ())), preferred_element_type=jnp.float32).astype(jnp.bfloat16)
    return (weight_update, first_new, second_new)
```

```python
import functools
import math

import jax
import jax.numpy as jnp
from jax import lax
from jax.experimental import pallas as pl
from jax.experimental.pallas import tpu as pltpu
from jax.sharding import PartitionSpec as P

NY, NZ = 8, 12
BLK = 20
RANK = 512
LANES = 128
G = RANK // LANES
PACK = G * BLK
KC = 8
F32, BF16 = jnp.float32, jnp.bfloat16
MESH = pl.DeviceIdType.MESH


def far_first(n):
    order = []
    for k in range(n // 2, 0, -1):
        order.append(k)
        if k != n - k:
            order.append(n - k)
    return order


def kernel(hid_hbm, og_hbm, bas_hbm, c1_hbm, s1_hbm, c2_hbm, s2_hbm,
           w_ref, m_ref, v_ref,
           hid, og, bas, c1, s1, c2, s2,
           htf, hperm, ht, acc, fac, proj, m_old, v_old,
           ring_y, ring_z, fresh_y, fresh_z, sumf, msg, land,
           stack, norm, gat, rowsf, bsel, wsend, wland,
           load_sem, send1, recv1, send2, recv2, send3, recv3, send4, recv4, *, tokens):
    dp, mp = lax.axis_index("dp"), lax.axis_index("mp")
    y, z = dp // NZ, dp % NZ
    core = mp % 2
    tok, ff = hid.shape
    kw = og.shape[2]

    def dev(yy, zz):
        return (yy * NZ + zz, mp)

    def at_y(k):
        return dev((y + k) % NY, z)

    def at_z(k):
        return dev(y, (z + k) % NZ)

    loads = [pltpu.make_async_copy(hid_hbm, hid, load_sem.at[0])]
    for k in range(KC):
        loads.append(pltpu.make_async_copy(og_hbm.at[:, pl.ds(k * kw, kw)], og.at[k], load_sem.at[1 + k]))
        loads.append(pltpu.make_async_copy(bas_hbm.at[pl.ds(k * kw, kw)], bas.at[pl.ds(k * kw, kw)], load_sem.at[1 + KC + k]))
    small = [(c1_hbm, c1), (s1_hbm, s1), (c2_hbm, c2), (s2_hbm, s2)]
    small = [pltpu.make_async_copy(a, b, load_sem.at[1 + 2 * KC + i]) for i, (a, b) in enumerate(small)]
    for c in loads + small:
        c.start()

    barrier = pltpu.get_barrier_semaphore()
    for k in range(1, NY):
        pl.semaphore_signal(barrier, inc=1, device_id=at_y(k), device_id_type=MESH)
    for k in range(1, NZ):
        pl.semaphore_signal(barrier, inc=1, device_id=at_z(k), device_id_type=MESH)

    loads[0].wait()
    for c in range(ff // LANES):
        htf[c * LANES:(c + 1) * LANES, :] = hid[:, c * LANES:(c + 1) * LANES].astype(F32).T

    @pl.when(core == 0)
    def _():
        ht[...] = htf[...].astype(BF16)

    @pl.when(core == 1)
    def _():
        for zz in range(NZ):
            for yy in range(NY):
                at = yy * NZ * BLK + zz * BLK
                hperm[yy * BLK:(yy + 1) * BLK, :] = htf[at:at + BLK, :]
            ht[zz * NY * BLK:(zz + 1) * NY * BLK, :] = hperm[...].astype(BF16)

    for k in range(KC):
        loads[1 + 2 * k].wait()
        loads[2 + 2 * k].wait()
        part = jnp.dot(og[k], bas[k * kw:(k + 1) * kw, :], preferred_element_type=F32)
        if k == 0:
            acc[...] = part
        elif k < KC - 1:
            acc[...] += part
        else:
            fac[...] = (acc[...] + part).astype(BF16)

    pl.semaphore_wait(barrier, NY - 1 + NZ - 1)

    def moments():
        for c in small:
            c.wait()
        eye = lax.broadcasted_iota(jnp.int32, (BLK, BLK), 0) == lax.broadcasted_iota(jnp.int32, (BLK, BLK), 1)
        half = RANK // 2
        for b in range(2):
            cols = slice(b * half, (b + 1) * half)
            sc1 = jnp.sum(jnp.where(eye, s1[b:b + 1, :], 0.0), axis=1, keepdims=True)
            sc2 = jnp.sum(jnp.where(eye, s2[b:b + 1, :], 0.0), axis=1, keepdims=True)
            m_old[:, cols] = 0.9 * (c1[:, cols].astype(F32) / 127.0 * sc1)
            v_old[:, cols] = 0.999 * ((c2[:, cols].astype(F32) / 255.0) ** 2 * sc2)

    def reduce_scatter(n1, n2, p1, p2, at1, at2, ring, fresh):
        rows = n2 * BLK
        half = n1 // 2
        pend = []

        def project(slot, d):
            block = ht[pl.ds(pl.multiple_of(d * rows, rows), rows), :]
            proj[slot, :rows, :] = jnp.dot(block, fac[...], preferred_element_type=F32)

        def lanes(g):
            return slice(g * LANES, (g + 1) * LANES)

        def hop(way, s, g, src):
            return pltpu.make_async_remote_copy(
                src_ref=src, dst_ref=ring.at[way * half + s, g],
                send_sem=send1.at[way, s, g], recv_sem=recv1.at[way, s, g],
                device_id=at1(1 if way == 0 else n1 - 1), device_id_type=MESH)

        def started(way, g):
            return (g < G // 2) == (way == 0)

        hops = {}
        project(0, (p1 + half) % n1)
        for g in range(G):
            way = 0 if g < G // 2 else 1
            fresh[way, g] = proj[0, :rows, lanes(g)].astype(BF16)
            c = hop(way, 0, g, fresh.at[way, g])
            c.start()
            hops[way, 0, g] = c
            pend.append(c)
        moments()
        for s in range(1, half):
            project(0, (p1 + half - s) % n1)
            project(1, (p1 + n1 - half + s) % n1)
            order = [g for g in range(G)]
            for i in range(G):
                for way in range(2):
                    g = order[i] if way == 0 else order[G - 1 - i]
                    val = proj[way, :rows, lanes(g)]
                    if s >= 2 or started(way, g):
                        hops[way, s - 1, g].wait_recv()
                        slot = ring.at[way * half + s - 1, g]
                        slot[...] = (val + slot[...].astype(F32)).astype(BF16)
                        c = hop(way, s, g, slot)
                    else:
                        fresh[way, g] = val.astype(BF16)
                        c = hop(way, s, g, fresh.at[way, g])
                    c.start()
                    hops[way, s, g] = c
                    pend.append(c)
        project(0, p1)
        for g in range(G):
            for way in range(2):
                hops[way, half - 1, g].wait_recv()
            val = (proj[0, :rows, lanes(g)] + ring[half - 1, g].astype(F32)) + ring[2 * half - 1, g].astype(F32)
            for j in range(n2):
                sumf[j * PACK + g * BLK:j * PACK + (g + 1) * BLK, :] = val[j * BLK:(j + 1) * BLK, :]
        msg[:n2] = sumf[:n2 * PACK, :].reshape(n2, PACK, LANES).astype(BF16)
        direct = []
        for k in far_first(n2):
            j = (p2 + k) % n2
            c = pltpu.make_async_remote_copy(
                src_ref=msg.at[j], dst_ref=land.at[k], send_sem=send2.at[k], recv_sem=recv2.at[k],
                device_id=at2(k), device_id_type=MESH)
            c.start()
            direct.append(c)
        total = sumf[pl.ds(pl.multiple_of(p2 * PACK, PACK), PACK), :]
        for i, k in reversed(list(enumerate(far_first(n2)))):
            direct[i].wait_recv()
            total = total + land[k].astype(F32)
        stack[...] = total
        for c in pend + direct:
            c.wait_send()

    @pl.when(core == 0)
    def _():
        reduce_scatter(NY, NZ, y, z, at_y, at_z, ring_y, fresh_y)

    @pl.when(core == 1)
    def _():
        reduce_scatter(NZ, NY, z, y, at_z, at_y, ring_z, fresh_z)

    for g in range(G):
        cols = slice(g * LANES, (g + 1) * LANES)
        low = stack[g * BLK:(g + 1) * BLK, :] / math.sqrt(tokens)
        first = m_old[:, cols] + 0.1 * low
        second = v_old[:, cols] + 0.001 * low * low
        m_ref[:, cols] = first
        v_ref[:, cols] = second
        norm[g * BLK:(g + 1) * BLK, :] = first / 0.19 / (jnp.sqrt(second / 0.001999) + 1e-8)
    gat[z] = norm[...].astype(BF16)

    pend = []
    for k in far_first(NZ):
        c = pltpu.make_async_remote_copy(
            src_ref=gat.at[z], dst_ref=gat.at[z], send_sem=send3.at[k], recv_sem=recv3.at[k],
            device_id=at_z(k), device_id_type=MESH)
        c.start()
        pend.append(c)
    for yy in range(NY):
        rows = pl.ds(pl.multiple_of((yy * NZ + z) * 64, 64), 64)
        bsel[yy * 64:(yy + 1) * 64, :] = bas[rows, :]
    for k in far_first(NZ)[::-1]:
        pltpu.make_async_remote_copy(
            src_ref=gat.at[z], dst_ref=gat.at[(z + NZ - k) % NZ], send_sem=send3.at[k], recv_sem=recv3.at[k],
            device_id=at_z(k), device_id_type=MESH).wait_recv()
    for zz in range(NZ):
        part = gat[zz].astype(F32)
        for g in range(G):
            rowsf[zz * BLK:(zz + 1) * BLK, g * LANES:(g + 1) * LANES] = part[g * BLK:(g + 1) * BLK, :]
    prod = lax.dot_general(bsel[...], rowsf[...].astype(BF16), (((1,), (1,)), ((), ())), preferred_element_type=F32)
    for yy in range(NY):
        wsend[yy] = prod[yy * 64:(yy + 1) * 64, :].astype(BF16)

    outs = []
    for k in far_first(NY):
        c = pltpu.make_async_remote_copy(
            src_ref=wsend.at[(y + k) % NY], dst_ref=wland.at[y], send_sem=send4.at[k], recv_sem=recv4.at[k],
            device_id=at_y(k), device_id_type=MESH)
        c.start()
        outs.append(c)
    wland[y] = wsend[y]
    for k in far_first(NY)[::-1]:
        pltpu.make_async_remote_copy(
            src_ref=wsend.at[y], dst_ref=wland.at[(y + NY - k) % NY], send_sem=send4.at[k], recv_sem=recv4.at[k],
            device_id=at_y(k), device_id_type=MESH).wait_recv()
    w_ref[...] = jnp.concatenate([wland[yy] for yy in range(NY)], axis=1)
    for c in pend + outs:
        c.wait_send()


def per_device(hidden_acts, out_grad, basis, code_first, scale_first, code_second, scale_second):
    tok, ff = hidden_acts.shape
    width = out_grad.shape[1]
    tokens = tok * lax.axis_size("dp")
    vm = pltpu.VMEM
    dma = pltpu.SemaphoreType.DMA
    any_spec = pl.BlockSpec(memory_space=pl.ANY)
    vmem_spec = pl.BlockSpec(memory_space=pltpu.VMEM)
    wt, first_new, second_new = pl.pallas_call(
        functools.partial(kernel, tokens=tokens),
        out_shape=(
            jax.ShapeDtypeStruct((64, ff), BF16),
            jax.ShapeDtypeStruct((BLK, RANK), F32),
            jax.ShapeDtypeStruct((BLK, RANK), F32),
        ),
        in_specs=[any_spec] * 7,
        out_specs=(vmem_spec,) * 3,
        scratch_shapes=[
            vm((tok, ff), BF16), vm((KC, tok, width // KC), BF16), vm((width, RANK), BF16),
            vm((BLK, RANK), jnp.int32), vm((2, BLK), F32), vm((BLK, RANK), jnp.int32), vm((2, BLK), F32),
            vm((ff, tok), F32), vm((NY * BLK, tok), F32), vm((ff, tok), BF16),
            vm((tok, RANK), F32), vm((tok, RANK), BF16), vm((2, NZ * BLK, RANK), F32),
            vm((BLK, RANK), F32), vm((BLK, RANK), F32),
            vm((NY, G, NZ * BLK, LANES), BF16), vm((NZ, G, NY * BLK, LANES), BF16),
            vm((2, G, NZ * BLK, LANES), BF16), vm((2, G, NY * BLK, LANES), BF16),
            vm((NZ * PACK, LANES), F32), vm((NZ, PACK, LANES), BF16), vm((NZ, PACK, LANES), BF16),
            vm((PACK, LANES), F32), vm((PACK, LANES), F32), vm((NZ, PACK, LANES), BF16),
            vm((NZ * BLK, RANK), F32), vm((NY * 64, RANK), BF16),
            vm((NY, 64, NZ * BLK), BF16), vm((NY, 64, NZ * BLK), BF16),
            dma((1 + 2 * KC + 4,)), dma((2, NZ // 2, G)), dma((2, NZ // 2, G)),
            dma((NZ,)), dma((NZ,)), dma((NZ,)), dma((NZ,)), dma((NY,)), dma((NY,)),
        ],
        compiler_params=pltpu.CompilerParams(
            collective_id=0, has_side_effects=True, vmem_limit_bytes=44 * 1024 * 1024),
    )(hidden_acts, out_grad, basis, code_first, scale_first.T, code_second, scale_second.T)
    return wt.T, first_new, second_new


def solution(mesh):
    state = P(("mp", "dp"), None)
    return jax.shard_map(
        per_device,
        mesh=mesh,
        in_specs=(P("dp", "mp"), P("dp", None), P(), state, state, state, state),
        out_specs=(P("mp", "dp"), state, state),
        check_vma=False,
    )
```

```python
import functools
import math

import jax
import jax.numpy as jnp
from jax import lax
from jax.experimental import pallas as pl
from jax.experimental.pallas import tpu as pltpu
from jax.sharding import PartitionSpec as P

NY, NZ = 8, 12
BLK = 20
RANK = 512
LANES = 128
COLS = 64
G = RANK // LANES
PACK = G * BLK
KC = 4
F32, BF16 = jnp.float32, jnp.bfloat16
MESH = pl.DeviceIdType.MESH


def far_first(n):
    order = []
    for k in range(n // 2, 0, -1):
        order.append(k)
        if k != n - k:
            order.append(n - k)
    return order


def kernel(hid_hbm, og_hbm, bas_hbm, c1_hbm, s1_hbm, c2_hbm, s2_hbm,
           w_ref, m_ref, v_ref,
           hid, og, bas, c1, s1, c2, s2,
           htf, hperm, ht, acc, acc_other, fac, proj, m_old, v_old,
           land_y, land_z, fresh_y, fresh_z, sumf, msg, land,
           stack, norm, gat, rowsf, bsel, wsend_y, wland_y, wsend_z, wland_z, wide,
           load_sem, send0, recv0, send1, recv1, send2, recv2, send3, recv3, send4, recv4, *, tokens):
    dp, mp = lax.axis_index("dp"), lax.axis_index("mp")
    y, z = dp // NZ, dp % NZ
    core = mp % 2
    tok, ff = hid.shape
    kw = og.shape[2]

    def dev(yy, zz):
        return (yy * NZ + zz, mp)

    def at_y(k):
        return dev((y + k) % NY, z)

    def at_z(k):
        return dev(y, (z + k) % NZ)

    loads = []
    base = core * (KC * kw)
    for k in range(KC):
        at = pl.ds(pl.multiple_of(base + k * kw, kw), kw)
        loads.append(pltpu.make_async_copy(og_hbm.at[:, at], og.at[k], load_sem.at[k]))
        loads.append(pltpu.make_async_copy(bas_hbm.at[at], bas.at[pl.ds(k * kw, kw)], load_sem.at[KC + k]))
    load_hid = pltpu.make_async_copy(hid_hbm, hid, load_sem.at[2 * KC])
    small = [(c1_hbm, c1), (s1_hbm, s1), (c2_hbm, c2), (s2_hbm, s2)]
    small = [pltpu.make_async_copy(a, b, load_sem.at[1 + 2 * KC + i]) for i, (a, b) in enumerate(small)]
    for c in loads + [load_hid] + small:
        c.start()

    barrier = pltpu.get_barrier_semaphore()
    for k in range(1, NY):
        pl.semaphore_signal(barrier, inc=1, device_id=at_y(k), device_id_type=MESH)
    for k in range(1, NZ):
        pl.semaphore_signal(barrier, inc=1, device_id=at_z(k), device_id_type=MESH)

    pl.semaphore_signal(barrier, inc=1, device_id=(dp, mp + 1 - 2 * core), device_id_type=MESH)

    swaps = []
    width = RANK // 2
    for k in range(KC):
        loads[2 * k].wait()
        loads[2 * k + 1].wait()
        for h in range(2):
            part = jnp.dot(og[k], bas[k * kw:(k + 1) * kw, h * width:(h + 1) * width], preferred_element_type=F32)
            acc[h] = part if k == 0 else acc[h] + part
            if k == KC - 1:
                if h == 0:
                    pl.semaphore_wait(barrier, NY - 1 + NZ - 1 + 1)
                c = pltpu.make_async_remote_copy(
                    src_ref=acc.at[h], dst_ref=acc_other.at[h], send_sem=send0.at[h], recv_sem=recv0.at[h],
                    device_id=(dp, mp + 1 - 2 * core), device_id_type=MESH)
                c.start()
                swaps.append(c)

    load_hid.wait()
    for c in range(ff // LANES):
        htf[c * LANES:(c + 1) * LANES, :] = hid[:, c * LANES:(c + 1) * LANES].astype(F32).T

    @pl.when(core == 0)
    def _():
        ht[...] = htf[...].astype(BF16)

    @pl.when(core == 1)
    def _():
        for zz in range(NZ):
            for yy in range(NY):
                at = yy * NZ * BLK + zz * BLK
                hperm[yy * BLK:(yy + 1) * BLK, :] = htf[at:at + BLK, :]
            ht[zz * NY * BLK:(zz + 1) * NY * BLK, :] = hperm[...].astype(BF16)

    for h in range(2):
        swaps[h].wait_recv()
        fac[:, h * width:(h + 1) * width] = (acc[h] + acc_other[h]).astype(BF16)

    late = []
    for yy in range(NY):
        late.append(pltpu.make_async_copy(
            bas_hbm.at[pl.ds(pl.multiple_of((yy * NZ + z) * COLS, COLS), COLS)],
            bsel.at[pl.ds(yy * COLS, COLS)], load_sem.at[2 * KC + 5 + yy]))
    late_z = pltpu.make_async_copy(
        bas_hbm.at[pl.ds(pl.multiple_of(y * NZ * COLS, COLS), NZ * COLS)], bsel, load_sem.at[2 * KC + 5])

    @pl.when(core == 0)
    def _():
        for c in late:
            c.start()

    @pl.when(core == 1)
    def _():
        late_z.start()

    def moments():
        for c in small:
            c.wait()
        eye = lax.broadcasted_iota(jnp.int32, (BLK, BLK), 0) == lax.broadcasted_iota(jnp.int32, (BLK, BLK), 1)
        half = RANK // 2
        for b in range(2):
            cols = slice(b * half, (b + 1) * half)
            sc1 = jnp.sum(jnp.where(eye, s1[b:b + 1, :], 0.0), axis=1, keepdims=True)
            sc2 = jnp.sum(jnp.where(eye, s2[b:b + 1, :], 0.0), axis=1, keepdims=True)
            m_old[:, cols] = 0.9 * (c1[:, cols].astype(F32) / 127.0 * sc1)
            v_old[:, cols] = 0.999 * ((c2[:, cols].astype(F32) / 255.0) ** 2 * sc2)

    def lanes(g):
        return slice(g * LANES, (g + 1) * LANES)

    def near(way, g):
        return (g < G // 2) == (way == 0)

    def project(slot, d, rows):
        block = ht[pl.ds(pl.multiple_of(d * rows, rows), rows), :]
        proj[slot, :rows, :] = jnp.dot(block, fac[...], preferred_element_type=F32)

    def ring_sum(rows):
        half = NY // 2
        pend, hops = [], {}

        def hop(way, s, g, src):
            c = pltpu.make_async_remote_copy(
                src_ref=src, dst_ref=land_y.at[way * half + s, g],
                send_sem=send1.at[way, s, g], recv_sem=recv1.at[way, s, g],
                device_id=at_y(1 if way == 0 else NY - 1), device_id_type=MESH)
            c.start()
            hops[way, s, g] = c
            pend.append(c)

        project(0, (y + half) % NY, rows)
        for g in range(G):
            way = 0 if near(0, g) else 1
            fresh_y[way, g] = proj[0, :rows, lanes(g)].astype(BF16)
            hop(way, 0, g, fresh_y.at[way, g])
        moments()
        for s in range(1, half):
            project(0, (y + half - s) % NY, rows)
            project(1, (y + half + s) % NY, rows)
            for i in range(G):
                for way in range(2):
                    g = i if way == 0 else G - 1 - i
                    val = proj[way, :rows, lanes(g)]
                    if s >= 2 or near(way, g):
                        hops[way, s - 1, g].wait_recv()
                        slot = land_y.at[way * half + s - 1, g]
                        slot[...] = (val + slot[...].astype(F32)).astype(BF16)
                        hop(way, s, g, slot)
                    else:
                        fresh_y[way, g] = val.astype(BF16)
                        hop(way, s, g, fresh_y.at[way, g])
        project(0, y, rows)
        for g in range(G):
            val = proj[0, :rows, lanes(g)]
            for way in range(2):
                hops[way, half - 1, g].wait_recv()
                val = val + land_y[way * half + half - 1, g].astype(F32)
            stacked(g, val, NZ)
        return pend

    def tree_sum(rows):
        pend, hops = [], {}

        def send(way, d, step, g, val):
            fresh_z[way, d - 1, g] = val.astype(BF16)
            c = pltpu.make_async_remote_copy(
                src_ref=fresh_z.at[way, d - 1, g], dst_ref=land_z.at[way, d - 1, g],
                send_sem=send1.at[way, d - 1, g], recv_sem=recv1.at[way, d - 1, g],
                device_id=at_z(step if way == 0 else NZ - step), device_id_type=MESH)
            c.start()
            hops[way, d, g] = c
            pend.append(c)

        def got(way, d, g):
            hops[way, d, g].wait_recv()
            return land_z[way, d - 1, g].astype(F32)

        def chunk(d):
            project(0, (z + d) % NZ, rows)
            project(1, (z + NZ - d) % NZ, rows)

        def leaf(d):
            chunk(d)
            for i in range(G):
                for way in range(2):
                    g = i if way == 0 else G - 1 - i
                    send(way, d, 1, g, proj[way, :rows, lanes(g)])

        def inner(d):
            chunk(d)
            for i in range(G):
                for way in range(2):
                    g = i if way == 0 else G - 1 - i
                    val = proj[way, :rows, lanes(g)] + got(way, d + 1, g)
                    if d + 2 < NZ // 2 or near(way, g):
                        val = val + got(way, d + 2, g)
                    send(way, d, 2, g, val)

        project(0, (z + NZ // 2) % NZ, rows)
        for g in (0, G - 1) + tuple(range(1, G - 1)):
            send(0 if near(0, g) else 1, NZ // 2, 2, g, proj[0, :rows, lanes(g)])
        leaf(5)
        leaf(3)
        moments()
        inner(4)
        leaf(1)
        inner(2)
        project(0, z, rows)
        for g in range(G):
            val = proj[0, :rows, lanes(g)]
            for d in (1, 2):
                for way in range(2):
                    val = val + got(way, d, g)
            stacked(g, val, NY)
        return pend

    def stacked(g, val, n2):
        for j in range(n2):
            sumf[j * PACK + g * BLK:j * PACK + (g + 1) * BLK, :] = val[j * BLK:(j + 1) * BLK, :]

    def direct_sum(n2, p2, at2, pend):
        msg[:n2] = sumf[:n2 * PACK, :].reshape(n2, PACK, LANES).astype(BF16)
        direct = []
        for k in far_first(n2):
            j = (p2 + k) % n2
            c = pltpu.make_async_remote_copy(
                src_ref=msg.at[j], dst_ref=land.at[k], send_sem=send2.at[k], recv_sem=recv2.at[k],
                device_id=at2(k), device_id_type=MESH)
            c.start()
            direct.append(c)
        total = sumf[pl.ds(pl.multiple_of(p2 * PACK, PACK), PACK), :]
        for i, k in reversed(list(enumerate(far_first(n2)))):
            direct[i].wait_recv()
            total = total + land[k].astype(F32)
        stack[...] = total
        for c in pend + direct:
            c.wait_send()

    @pl.when(core == 0)
    def _():
        direct_sum(NZ, z, at_z, ring_sum(NZ * BLK))

    @pl.when(core == 1)
    def _():
        direct_sum(NY, y, at_y, tree_sum(NY * BLK))

    for g in range(G):
        cols = slice(g * LANES, (g + 1) * LANES)
        low = stack[g * BLK:(g + 1) * BLK, :] / math.sqrt(tokens)
        first = m_old[:, cols] + 0.1 * low
        second = v_old[:, cols] + 0.001 * low * low
        m_ref[:, cols] = first
        v_ref[:, cols] = second
        norm[g * BLK:(g + 1) * BLK, :] = first / 0.19 / (jnp.sqrt(second / 0.001999) + 1e-8)

    def gather(n, p, at):
        gat[p] = norm[...].astype(BF16)
        sends = []
        for k in far_first(n):
            c = pltpu.make_async_remote_copy(
                src_ref=gat.at[p], dst_ref=gat.at[p], send_sem=send3.at[k], recv_sem=recv3.at[k],
                device_id=at(k), device_id_type=MESH)
            c.start()
            sends.append(c)
        for k in far_first(n)[::-1]:
            pltpu.make_async_remote_copy(
                src_ref=gat.at[p], dst_ref=gat.at[(p + n - k) % n], send_sem=send3.at[k], recv_sem=recv3.at[k],
                device_id=at(k), device_id_type=MESH).wait_recv()
        for b in range(n):
            part = gat[b].astype(F32)
            for g in range(G):
                rowsf[b * BLK:(b + 1) * BLK, g * LANES:(g + 1) * LANES] = part[g * BLK:(g + 1) * BLK, :]
        return sends

    def exchange(n, p, at, src, dst):
        sends = []
        for k in far_first(n):
            c = pltpu.make_async_remote_copy(
                src_ref=src.at[(p + k) % n], dst_ref=dst.at[p], send_sem=send4.at[k], recv_sem=recv4.at[k],
                device_id=at(k), device_id_type=MESH)
            c.start()
            sends.append(c)
        dst[p] = src[p]
        for k in far_first(n)[::-1]:
            pltpu.make_async_remote_copy(
                src_ref=src.at[p], dst_ref=dst.at[(p + n - k) % n], send_sem=send4.at[k], recv_sem=recv4.at[k],
                device_id=at(k), device_id_type=MESH).wait_recv()
        return sends

    nt = (((1,), (1,)), ((), ()))

    @pl.when(core == 0)
    def _():
        sends = gather(NZ, z, at_z)
        for c in late:
            c.wait()
        prod = lax.dot_general(bsel[:NY * COLS, :], rowsf[...].astype(BF16), nt, preferred_element_type=F32)
        for yy in range(NY):
            wsend_y[yy] = prod[yy * COLS:(yy + 1) * COLS, :].astype(BF16)
        sends += exchange(NY, y, at_y, wsend_y, wland_y)
        w_ref[...] = jnp.concatenate([wland_y[yy] for yy in range(NY)], axis=1)
        for c in sends:
            c.wait_send()

    @pl.when(core == 1)
    def _():
        sends = gather(NY, y, at_y)
        late_z.wait()
        part = NY // 2 * BLK
        rows = rowsf[:NY * BLK, :].astype(BF16)
        left = lax.broadcasted_iota(jnp.int32, (part, LANES), 1) < COLS
        for q in range(NZ // 2):
            pair = lax.dot_general(rows, bsel[q * LANES:(q + 1) * LANES, :], nt, preferred_element_type=F32)
            low, high = pair[:part, :], pair[part:, :]
            wsend_z[2 * q] = jnp.where(left, low, pltpu.roll(high, COLS, 1)).astype(BF16)
            wsend_z[2 * q + 1] = jnp.where(left, pltpu.roll(low, COLS, 1), high).astype(BF16)
        sends += exchange(NZ, z, at_z, wsend_z, wland_z)
        for zz in range(NZ):
            got = wland_z[zz].astype(F32)
            for b in range(NY // 2):
                at = b * NZ * BLK + zz * BLK
                wide[at:at + BLK, :] = got[b * BLK:(b + 1) * BLK, :]
        wt = wide[...].T.astype(BF16)
        w_ref[...] = jnp.concatenate([wt[:COLS, :], wt[COLS:, :]], axis=1)
        for c in sends:
            c.wait_send()

    for c in swaps:
        c.wait_send()


def per_device(hidden_acts, out_grad, basis, code_first, scale_first, code_second, scale_second):
    tok, ff = hidden_acts.shape
    width = out_grad.shape[1]
    tokens = tok * lax.axis_size("dp")
    vm = pltpu.VMEM
    dma = pltpu.SemaphoreType.DMA
    any_spec = pl.BlockSpec(memory_space=pl.ANY)
    vmem_spec = pl.BlockSpec(memory_space=pltpu.VMEM)
    wt, first_new, second_new = pl.pallas_call(
        functools.partial(kernel, tokens=tokens),
        out_shape=(
            jax.ShapeDtypeStruct((COLS, ff), BF16),
            jax.ShapeDtypeStruct((BLK, RANK), F32),
            jax.ShapeDtypeStruct((BLK, RANK), F32),
        ),
        in_specs=[any_spec] * 7,
        out_specs=(vmem_spec,) * 3,
        scratch_shapes=[
            vm((tok, ff), BF16), vm((KC, tok, width // 2 // KC), BF16), vm((width // 2, RANK), BF16),
            vm((BLK, RANK), jnp.int32), vm((2, BLK), F32), vm((BLK, RANK), jnp.int32), vm((2, BLK), F32),
            vm((ff, tok), F32), vm((NY * BLK, tok), F32), vm((ff, tok), BF16),
            vm((2, tok, RANK // 2), F32), vm((2, tok, RANK // 2), F32), vm((tok, RANK), BF16), vm((2, NZ * BLK, RANK), F32),
            vm((BLK, RANK), F32), vm((BLK, RANK), F32),
            vm((NY, G, NZ * BLK, LANES), BF16), vm((2, NZ // 2, G, NY * BLK, LANES), BF16),
            vm((2, G, NZ * BLK, LANES), BF16), vm((2, NZ // 2, G, NY * BLK, LANES), BF16),
            vm((NZ * PACK, LANES), F32), vm((NZ, PACK, LANES), BF16), vm((NZ, PACK, LANES), BF16),
            vm((PACK, LANES), F32), vm((PACK, LANES), F32), vm((NZ, PACK, LANES), BF16),
            vm((NZ * BLK, RANK), F32), vm((NZ * COLS, RANK), BF16),
            vm((NY, COLS, NZ * BLK), BF16), vm((NY, COLS, NZ * BLK), BF16),
            vm((NZ, PACK, LANES), BF16), vm((NZ, PACK, LANES), BF16), vm((ff // 2, LANES), F32),
            dma((2 * KC + 5 + NY,)), dma((2,)), dma((2,)), dma((2, NZ // 2, G)), dma((2, NZ // 2, G)),
            dma((NZ,)), dma((NZ,)), dma((NZ,)), dma((NZ,)), dma((NZ,)), dma((NZ,)),
        ],
        compiler_params=pltpu.CompilerParams(
            collective_id=0, has_side_effects=True, vmem_limit_bytes=44 * 1024 * 1024),
    )(*[pltpu.with_memory_space_constraint(a, pltpu.HBM) for a in (hidden_acts, out_grad, basis, code_first, scale_first.T, code_second, scale_second.T)])
    return wt.T, first_new, second_new


def solution(mesh):
    state = P(("mp", "dp"), None)
    return jax.shard_map(
        per_device,
        mesh=mesh,
        in_specs=(P("dp", "mp"), P("dp", None), P(), state, state, state, state),
        out_specs=(P("mp", "dp"), state, state),
        check_vma=False,
    )
```

```python
import functools
import math

import jax
import jax.numpy as jnp
from jax import lax
from jax.experimental import pallas as pl
from jax.experimental.pallas import tpu as pltpu
from jax.sharding import PartitionSpec as P

NY, NZ = 8, 12
BLK = 20
RANK = 512
LANES = 128
COLS = 64
G = RANK // LANES
PACK = G * BLK
KC = 4
F32, BF16 = jnp.float32, jnp.bfloat16
MESH = pl.DeviceIdType.MESH


def far_first(n):
    order = []
    for k in range(n // 2, 0, -1):
        order.append(k)
        if k != n - k:
            order.append(n - k)
    return order


def kernel(hid_hbm, og_hbm, bas_hbm, c1_hbm, s1_hbm, c2_hbm, s2_hbm,
           w_ref, m_ref, v_ref,
           hid, og, bas, c1, s1, c2, s2,
           htf, hperm, ht, acc, acc_other, fac, proj, m_old, v_old,
           land_y, land_z, fresh_y, fresh_z, sumf, msg, land,
           stack, norm, gat, rowsf, bsel, wsend_y, wland_y, wsend_z, wland_z, wide,
           load_sem, send0, recv0, send1, recv1, send2, recv2, send3, recv3, send4, recv4, *, tokens):
    dp, mp = lax.axis_index("dp"), lax.axis_index("mp")
    y, z = dp // NZ, dp % NZ
    core = mp % 2
    tok, ff = hid.shape
    kw = og.shape[2]

    def dev(yy, zz):
        return (yy * NZ + zz, mp)

    def at_y(k):
        return dev((y + k) % NY, z)

    def at_z(k):
        return dev(y, (z + k) % NZ)

    loads = []
    base = core * (KC * kw)
    for k in range(KC):
        at = pl.ds(pl.multiple_of(base + k * kw, kw), kw)
        loads.append(pltpu.make_async_copy(og_hbm.at[:, at], og.at[k], load_sem.at[k]))
        loads.append(pltpu.make_async_copy(bas_hbm.at[at], bas.at[pl.ds(k * kw, kw)], load_sem.at[KC + k]))
    load_hid = pltpu.make_async_copy(hid_hbm, hid, load_sem.at[2 * KC])
    small = [(c1_hbm, c1), (s1_hbm, s1), (c2_hbm, c2), (s2_hbm, s2)]
    small = [pltpu.make_async_copy(a, b, load_sem.at[1 + 2 * KC + i]) for i, (a, b) in enumerate(small)]
    for c in loads + [load_hid] + small:
        c.start()

    barrier = pltpu.get_barrier_semaphore()
    for k in range(1, NY):
        pl.semaphore_signal(barrier, inc=1, device_id=at_y(k), device_id_type=MESH)
    for k in range(1, NZ):
        pl.semaphore_signal(barrier, inc=1, device_id=at_z(k), device_id_type=MESH)

    pl.semaphore_signal(barrier, inc=1, device_id=(dp, mp + 1 - 2 * core), device_id_type=MESH)

    swaps = []
    width = RANK // 2
    for k in range(KC):
        loads[2 * k].wait()
        loads[2 * k + 1].wait()
        for h in range(2):
            part = jnp.dot(og[k], bas[k * kw:(k + 1) * kw, h * width:(h + 1) * width], preferred_element_type=F32)
            acc[h] = part if k == 0 else acc[h] + part
            if k == KC - 1:
                if h == 0:
                    pl.semaphore_wait(barrier, NY - 1 + NZ - 1 + 1)
                c = pltpu.make_async_remote_copy(
                    src_ref=acc.at[h], dst_ref=acc_other.at[h], send_sem=send0.at[h], recv_sem=recv0.at[h],
                    device_id=(dp, mp + 1 - 2 * core), device_id_type=MESH)
                c.start()
                swaps.append(c)

    load_hid.wait()
    for c in range(ff // LANES):
        htf[c * LANES:(c + 1) * LANES, :] = hid[:, c * LANES:(c + 1) * LANES].astype(F32).T

    @pl.when(core == 0)
    def _():
        ht[...] = htf[...].astype(BF16)

    @pl.when(core == 1)
    def _():
        for zz in range(NZ):
            for yy in range(NY):
                at = yy * NZ * BLK + zz * BLK
                hperm[yy * BLK:(yy + 1) * BLK, :] = htf[at:at + BLK, :]
            ht[zz * NY * BLK:(zz + 1) * NY * BLK, :] = hperm[...].astype(BF16)

    for h in range(2):
        swaps[h].wait_recv()
        fac[:, h * width:(h + 1) * width] = (acc[h] + acc_other[h]).astype(BF16)

    late = []
    for yy in range(NY):
        late.append(pltpu.make_async_copy(
            bas_hbm.at[pl.ds(pl.multiple_of((yy * NZ + z) * COLS, COLS), COLS)],
            bsel.at[pl.ds(yy * COLS, COLS)], load_sem.at[2 * KC + 5 + yy]))
    late_z = pltpu.make_async_copy(
        bas_hbm.at[pl.ds(pl.multiple_of(y * NZ * COLS, COLS), NZ * COLS)], bsel, load_sem.at[2 * KC + 5])

    @pl.when(core == 0)
    def _():
        for c in late:
            c.start()

    @pl.when(core == 1)
    def _():
        late_z.start()

    def moments():
        for c in small:
            c.wait()
        eye = lax.broadcasted_iota(jnp.int32, (BLK, BLK), 0) == lax.broadcasted_iota(jnp.int32, (BLK, BLK), 1)
        half = RANK // 2
        for b in range(2):
            cols = slice(b * half, (b + 1) * half)
            sc1 = jnp.sum(jnp.where(eye, s1[b:b + 1, :], 0.0), axis=1, keepdims=True)
            sc2 = jnp.sum(jnp.where(eye, s2[b:b + 1, :], 0.0), axis=1, keepdims=True)
            m_old[:, cols] = 0.9 * (c1[:, cols].astype(F32) / 127.0 * sc1)
            v_old[:, cols] = 0.999 * ((c2[:, cols].astype(F32) / 255.0) ** 2 * sc2)

    def lanes(g):
        return slice(g * LANES, (g + 1) * LANES)

    def near(way, g):
        return (g < G // 2) == (way == 0)

    def project(slot, d, rows):
        block = ht[pl.ds(pl.multiple_of(d * rows, rows), rows), :]
        proj[slot, :rows, :] = jnp.dot(block, fac[...], preferred_element_type=F32)

    def ring_sum(rows):
        half = NY // 2
        pend, hops = [], {}

        def hop(way, s, g, src):
            c = pltpu.make_async_remote_copy(
                src_ref=src, dst_ref=land_y.at[way * half + s, g],
                send_sem=send1.at[way, s, g], recv_sem=recv1.at[way, s, g],
                device_id=at_y(1 if way == 0 else NY - 1), device_id_type=MESH)
            c.start()
            hops[way, s, g] = c
            pend.append(c)

        project(0, (y + half) % NY, rows)
        for g in range(G):
            way = 0 if near(0, g) else 1
            fresh_y[way, g] = proj[0, :rows, lanes(g)].astype(BF16)
            hop(way, 0, g, fresh_y.at[way, g])
        moments()
        for s in range(1, half):
            project(0, (y + half - s) % NY, rows)
            project(1, (y + half + s) % NY, rows)
            for i in range(G):
                for way in range(2):
                    g = i if way == 0 else G - 1 - i
                    val = proj[way, :rows, lanes(g)]
                    if s >= 2 or near(way, g):
                        hops[way, s - 1, g].wait_recv()
                        slot = land_y.at[way * half + s - 1, g]
                        slot[...] = (val + slot[...].astype(F32)).astype(BF16)
                        hop(way, s, g, slot)
                    else:
                        fresh_y[way, g] = val.astype(BF16)
                        hop(way, s, g, fresh_y.at[way, g])
        project(0, y, rows)
        for g in range(G):
            val = proj[0, :rows, lanes(g)]
            for way in range(2):
                hops[way, half - 1, g].wait_recv()
                val = val + land_y[way * half + half - 1, g].astype(F32)
            stacked(g, val, NZ)
        return pend

    def tree_sum(rows):
        pend, hops = [], {}

        def send(way, d, step, g, val):
            fresh_z[way, d - 1, g] = val.astype(BF16)
            c = pltpu.make_async_remote_copy(
                src_ref=fresh_z.at[way, d - 1, g], dst_ref=land_z.at[way, d - 1, g],
                send_sem=send1.at[way, d - 1, g], recv_sem=recv1.at[way, d - 1, g],
                device_id=at_z(step if way == 0 else NZ - step), device_id_type=MESH)
            c.start()
            hops[way, d, g] = c
            pend.append(c)

        def got(way, d, g):
            hops[way, d, g].wait_recv()
            return land_z[way, d - 1, g].astype(F32)

        def chunk(d):
            project(0, (z + d) % NZ, rows)
            project(1, (z + NZ - d) % NZ, rows)

        def leaf(d):
            chunk(d)
            for i in range(G):
                for way in range(2):
                    g = i if way == 0 else G - 1 - i
                    send(way, d, 1, g, proj[way, :rows, lanes(g)])

        def inner(d):
            chunk(d)
            for i in range(G):
                for way in range(2):
                    g = i if way == 0 else G - 1 - i
                    val = proj[way, :rows, lanes(g)] + got(way, d + 1, g)
                    if d + 2 < NZ // 2 or near(way, g):
                        val = val + got(way, d + 2, g)
                    send(way, d, 2, g, val)

        project(0, (z + NZ // 2) % NZ, rows)
        for g in (0, G - 1) + tuple(range(1, G - 1)):
            send(0 if near(0, g) else 1, NZ // 2, 2, g, proj[0, :rows, lanes(g)])
        leaf(5)
        leaf(3)
        moments()
        inner(4)
        leaf(1)
        inner(2)
        project(0, z, rows)
        for g in range(G):
            val = proj[0, :rows, lanes(g)]
            for d in (1, 2):
                for way in range(2):
                    val = val + got(way, d, g)
            stacked(g, val, NY)
        return pend

    def stacked(g, val, n2):
        for j in range(n2):
            sumf[j * PACK + g * BLK:j * PACK + (g + 1) * BLK, :] = val[j * BLK:(j + 1) * BLK, :]

    def direct_sum(n2, p2, at2, pend):
        msg[:n2] = sumf[:n2 * PACK, :].reshape(n2, PACK, LANES).astype(BF16)
        direct = []
        for k in far_first(n2):
            j = (p2 + k) % n2
            c = pltpu.make_async_remote_copy(
                src_ref=msg.at[j], dst_ref=land.at[k], send_sem=send2.at[k], recv_sem=recv2.at[k],
                device_id=at2(k), device_id_type=MESH)
            c.start()
            direct.append(c)
        total = sumf[pl.ds(pl.multiple_of(p2 * PACK, PACK), PACK), :]
        for i, k in reversed(list(enumerate(far_first(n2)))):
            direct[i].wait_recv()
            total = total + land[k].astype(F32)
        stack[...] = total
        return pend + direct

    def adam():
        for g in range(G):
            cols = slice(g * LANES, (g + 1) * LANES)
            low = stack[g * BLK:(g + 1) * BLK, :] / math.sqrt(tokens)
            first = m_old[:, cols] + 0.1 * low
            second = v_old[:, cols] + 0.001 * low * low
            m_ref[:, cols] = first
            v_ref[:, cols] = second
            norm[g * BLK:(g + 1) * BLK, :] = first / 0.19 / (jnp.sqrt(second / 0.001999) + 1e-8)

    def gather(n, p, at):
        gat[p] = norm[...].astype(BF16)
        sends = []
        for k in far_first(n):
            c = pltpu.make_async_remote_copy(
                src_ref=gat.at[p], dst_ref=gat.at[p], send_sem=send3.at[k], recv_sem=recv3.at[k],
                device_id=at(k), device_id_type=MESH)
            c.start()
            sends.append(c)
        for k in far_first(n)[::-1]:
            pltpu.make_async_remote_copy(
                src_ref=gat.at[p], dst_ref=gat.at[(p + n - k) % n], send_sem=send3.at[k], recv_sem=recv3.at[k],
                device_id=at(k), device_id_type=MESH).wait_recv()
        for b in range(n):
            part = gat[b].astype(F32)
            for g in range(G):
                rowsf[b * BLK:(b + 1) * BLK, g * LANES:(g + 1) * LANES] = part[g * BLK:(g + 1) * BLK, :]
        return sends

    def exchange(n, p, at, src, dst):
        sends = []
        for k in far_first(n):
            c = pltpu.make_async_remote_copy(
                src_ref=src.at[(p + k) % n], dst_ref=dst.at[p], send_sem=send4.at[k], recv_sem=recv4.at[k],
                device_id=at(k), device_id_type=MESH)
            c.start()
            sends.append(c)
        dst[p] = src[p]
        for k in far_first(n)[::-1]:
            pltpu.make_async_remote_copy(
                src_ref=src.at[p], dst_ref=dst.at[(p + n - k) % n], send_sem=send4.at[k], recv_sem=recv4.at[k],
                device_id=at(k), device_id_type=MESH).wait_recv()
        return sends

    nt = (((1,), (1,)), ((), ()))

    @pl.when(core == 0)
    def _():
        sends = direct_sum(NZ, z, at_z, ring_sum(NZ * BLK))
        adam()
        sends += gather(NZ, z, at_z)
        for c in late:
            c.wait()
        prod = lax.dot_general(bsel[:NY * COLS, :], rowsf[...].astype(BF16), nt, preferred_element_type=F32)
        for yy in range(NY):
            wsend_y[yy] = prod[yy * COLS:(yy + 1) * COLS, :].astype(BF16)
        sends += exchange(NY, y, at_y, wsend_y, wland_y)
        w_ref[...] = jnp.concatenate([wland_y[yy] for yy in range(NY)], axis=1)
        for c in sends:
            c.wait_send()

    @pl.when(core == 1)
    def _():
        sends = direct_sum(NY, y, at_y, tree_sum(NY * BLK))
        adam()
        sends += gather(NY, y, at_y)
        late_z.wait()
        part = NY // 2 * BLK
        rows = rowsf[:NY * BLK, :].astype(BF16)
        left = lax.broadcasted_iota(jnp.int32, (part, LANES), 1) < COLS
        for q in range(NZ // 2):
            pair = lax.dot_general(rows, bsel[q * LANES:(q + 1) * LANES, :], nt, preferred_element_type=F32)
            low, high = pair[:part, :], pair[part:, :]
            wsend_z[2 * q] = jnp.where(left, low, pltpu.roll(high, COLS, 1)).astype(BF16)
            wsend_z[2 * q + 1] = jnp.where(left, pltpu.roll(low, COLS, 1), high).astype(BF16)
        sends += exchange(NZ, z, at_z, wsend_z, wland_z)
        for zz in range(NZ):
            got = wland_z[zz].astype(F32)
            for b in range(NY // 2):
                at = b * NZ * BLK + zz * BLK
                wide[at:at + BLK, :] = got[b * BLK:(b + 1) * BLK, :]
        wt = wide[...].T.astype(BF16)
        w_ref[...] = jnp.concatenate([wt[:COLS, :], wt[COLS:, :]], axis=1)
        for c in sends:
            c.wait_send()

    for c in swaps:
        c.wait_send()


def store(wt, first_new, second_new, wt_out, first_out, second_out, sem):
    pairs = ((wt, wt_out), (first_new, first_out), (second_new, second_out))
    copies = [pltpu.make_async_copy(a, b, sem.at[i]) for i, (a, b) in enumerate(pairs)]
    for c in copies:
        c.start()
    for c in copies:
        c.wait()


def per_device(hidden_acts, out_grad, basis, code_first, scale_first, code_second, scale_second):
    tok, ff = hidden_acts.shape
    width = out_grad.shape[1]
    tokens = tok * lax.axis_size("dp")
    vm = pltpu.VMEM
    dma = pltpu.SemaphoreType.DMA
    any_spec = pl.BlockSpec(memory_space=pl.ANY)
    vmem_spec = pl.BlockSpec(memory_space=pltpu.VMEM)
    wt, first_new, second_new = pl.pallas_call(
        functools.partial(kernel, tokens=tokens),
        out_shape=(
            jax.ShapeDtypeStruct((COLS, ff), BF16),
            jax.ShapeDtypeStruct((BLK, RANK), F32),
            jax.ShapeDtypeStruct((BLK, RANK), F32),
        ),
        in_specs=[any_spec] * 7,
        out_specs=(vmem_spec,) * 3,
        scratch_shapes=[
            vm((tok, ff), BF16), vm((KC, tok, width // 2 // KC), BF16), vm((width // 2, RANK), BF16),
            vm((BLK, RANK), jnp.int32), vm((2, BLK), F32), vm((BLK, RANK), jnp.int32), vm((2, BLK), F32),
            vm((ff, tok), F32), vm((NY * BLK, tok), F32), vm((ff, tok), BF16),
            vm((2, tok, RANK // 2), F32), vm((2, tok, RANK // 2), F32), vm((tok, RANK), BF16), vm((2, NZ * BLK, RANK), F32),
            vm((BLK, RANK), F32), vm((BLK, RANK), F32),
            vm((NY, G, NZ * BLK, LANES), BF16), vm((2, NZ // 2, G, NY * BLK, LANES), BF16),
            vm((2, G, NZ * BLK, LANES), BF16), vm((2, NZ // 2, G, NY * BLK, LANES), BF16),
            vm((NZ * PACK, LANES), F32), vm((NZ, PACK, LANES), BF16), vm((NZ, PACK, LANES), BF16),
            vm((PACK, LANES), F32), vm((PACK, LANES), F32), vm((NZ, PACK, LANES), BF16),
            vm((NZ * BLK, RANK), F32), vm((NZ * COLS, RANK), BF16),
            vm((NY, COLS, NZ * BLK), BF16), vm((NY, COLS, NZ * BLK), BF16),
            vm((NZ, PACK, LANES), BF16), vm((NZ, PACK, LANES), BF16), vm((ff // 2, LANES), F32),
            dma((2 * KC + 5 + NY,)), dma((2,)), dma((2,)), dma((2, NZ // 2, G)), dma((2, NZ // 2, G)),
            dma((NZ,)), dma((NZ,)), dma((NZ,)), dma((NZ,)), dma((NZ,)), dma((NZ,)),
        ],
        compiler_params=pltpu.CompilerParams(
            collective_id=0, has_side_effects=True, vmem_limit_bytes=44 * 1024 * 1024),
    )(*[pltpu.with_memory_space_constraint(a, pltpu.HBM) for a in (hidden_acts, out_grad, basis, code_first, scale_first.T, code_second, scale_second.T)])
    wt, first_new, second_new = pl.pallas_call(
        store,
        out_shape=[jax.ShapeDtypeStruct(a.shape, a.dtype) for a in (wt, first_new, second_new)],
        in_specs=[any_spec] * 3,
        out_specs=[any_spec] * 3,
        scratch_shapes=[dma((3,))],
        compiler_params=pltpu.CompilerParams(vmem_limit_bytes=1024 * 1024),
    )(wt, first_new, second_new)
    return wt.T, first_new, second_new


def solution(mesh):
    state = P(("mp", "dp"), None)
    return jax.shard_map(
        per_device,
        mesh=mesh,
        in_specs=(P("dp", "mp"), P("dp", None), P(), state, state, state, state),
        out_specs=(P("mp", "dp"), state, state),
        check_vma=False,
    )
```

```python
import functools
import math

import jax
import jax.numpy as jnp
from jax import lax
from jax.experimental import pallas as pl
from jax.experimental.pallas import tpu as pltpu
from jax.sharding import PartitionSpec as P

NY, NZ = 8, 12
BLK = 20
RANK = 512
LANES = 128
COLS = 64
G = RANK // LANES
PACK = G * BLK
KC = 4
F32, BF16 = jnp.float32, jnp.bfloat16
MESH = pl.DeviceIdType.MESH


def far_first(n):
    order = []
    for k in range(n // 2, 0, -1):
        order.append(k)
        if k != n - k:
            order.append(n - k)
    return order


def kernel(hid_hbm, og_hbm, bas_hbm, c1_hbm, s1_hbm, c2_hbm, s2_hbm,
           w_ref, m_ref, v_ref,
           hid, og, bas, c1, s1, c2, s2,
           htf, hperm, ht, acc, acc_other, fac, proj, m_old, v_old,
           land_y, land_z, fresh_y, fresh_z, sumf, msg, land,
           stack, norm, gat, rowsf, bsel, wsend_y, wland_y, wsend_z, wland_z, wide,
           load_sem, send0, recv0, send1, recv1, send2, recv2, send3, recv3, send4, recv4, *, tokens):
    dp, mp = lax.axis_index("dp"), lax.axis_index("mp")
    y, z = dp // NZ, dp % NZ
    core = mp % 2
    tok, ff = hid.shape
    kw = og.shape[2]

    def dev(yy, zz):
        return (yy * NZ + zz, mp)

    def at_y(k):
        return dev((y + k) % NY, z)

    def at_z(k):
        return dev(y, (z + k) % NZ)

    loads = []
    base = core * (KC * kw)
    for k in range(KC):
        at = pl.ds(pl.multiple_of(base + k * kw, kw), kw)
        loads.append(pltpu.make_async_copy(og_hbm.at[:, at], og.at[k], load_sem.at[k]))
        loads.append(pltpu.make_async_copy(bas_hbm.at[at], bas.at[pl.ds(k * kw, kw)], load_sem.at[KC + k]))
    load_hid = pltpu.make_async_copy(hid_hbm, hid, load_sem.at[2 * KC])
    small = [(c1_hbm, c1), (s1_hbm, s1), (c2_hbm, c2), (s2_hbm, s2)]
    small = [pltpu.make_async_copy(a, b, load_sem.at[1 + 2 * KC + i]) for i, (a, b) in enumerate(small)]
    for c in loads[:-2] + [load_hid] + loads[-2:]:
        c.start()

    barrier = pltpu.get_barrier_semaphore()
    for k in far_first(NY):
        pl.semaphore_signal(barrier, inc=1, device_id=at_y(k), device_id_type=MESH)
    for k in far_first(NZ):
        pl.semaphore_signal(barrier, inc=1, device_id=at_z(k), device_id_type=MESH)

    pl.semaphore_signal(barrier, inc=1, device_id=(dp, mp + 1 - 2 * core), device_id_type=MESH)

    for c in small:
        c.start()

    def transpose_hidden():
        load_hid.wait()
        for c in range(ff // LANES):
            htf[c * LANES:(c + 1) * LANES, :] = hid[:, c * LANES:(c + 1) * LANES].astype(F32).T

        @pl.when(core == 0)
        def _():
            ht[...] = htf[...].astype(BF16)

        @pl.when(core == 1)
        def _():
            for zz in range(NZ):
                for yy in range(NY):
                    at = yy * NZ * BLK + zz * BLK
                    hperm[yy * BLK:(yy + 1) * BLK, :] = htf[at:at + BLK, :]
                ht[zz * NY * BLK:(zz + 1) * NY * BLK, :] = hperm[...].astype(BF16)

    swaps = []
    width = RANK // 2
    for k in range(KC):
        if k == KC - 1:
            transpose_hidden()
        loads[2 * k].wait()
        loads[2 * k + 1].wait()
        for h in range(2):
            part = jnp.dot(og[k], bas[k * kw:(k + 1) * kw, h * width:(h + 1) * width], preferred_element_type=F32)
            acc[h] = part if k == 0 else acc[h] + part
            if k == KC - 1:
                if h == 0:
                    pl.semaphore_wait(barrier, NY - 1 + NZ - 1 + 1)
                c = pltpu.make_async_remote_copy(
                    src_ref=acc.at[h], dst_ref=acc_other.at[h], send_sem=send0.at[h], recv_sem=recv0.at[h],
                    device_id=(dp, mp + 1 - 2 * core), device_id_type=MESH)
                c.start()
                swaps.append(c)

    for h in range(2):
        swaps[h].wait_recv()
        fac[:, h * width:(h + 1) * width] = (acc[h] + acc_other[h]).astype(BF16)

    late = []
    for yy in range(NY):
        late.append(pltpu.make_async_copy(
            bas_hbm.at[pl.ds(pl.multiple_of((yy * NZ + z) * COLS, COLS), COLS)],
            bsel.at[pl.ds(yy * COLS, COLS)], load_sem.at[2 * KC + 5 + yy]))
    late_z = pltpu.make_async_copy(
        bas_hbm.at[pl.ds(pl.multiple_of(y * NZ * COLS, COLS), NZ * COLS)], bsel, load_sem.at[2 * KC + 5])

    @pl.when(core == 0)
    def _():
        for c in late:
            c.start()

    @pl.when(core == 1)
    def _():
        late_z.start()

    def moments():
        for c in small:
            c.wait()
        eye = lax.broadcasted_iota(jnp.int32, (BLK, BLK), 0) == lax.broadcasted_iota(jnp.int32, (BLK, BLK), 1)
        half = RANK // 2
        for b in range(2):
            cols = slice(b * half, (b + 1) * half)
            sc1 = jnp.sum(jnp.where(eye, s1[b:b + 1, :], 0.0), axis=1, keepdims=True)
            sc2 = jnp.sum(jnp.where(eye, s2[b:b + 1, :], 0.0), axis=1, keepdims=True)
            m_old[:, cols] = 0.9 * (c1[:, cols].astype(F32) / 127.0 * sc1)
            v_old[:, cols] = 0.999 * ((c2[:, cols].astype(F32) / 255.0) ** 2 * sc2)

    def lanes(g):
        return slice(g * LANES, (g + 1) * LANES)

    def near(way, g):
        return (g < G // 2) == (way == 0)

    def project(slot, d, rows):
        block = ht[pl.ds(pl.multiple_of(d * rows, rows), rows), :]
        proj[slot, :rows, :] = jnp.dot(block, fac[...], preferred_element_type=F32)

    def tree_sum(n, p, at, fresh, land, rows, n2, plan):
        pend, hops = [], {}

        def send(way, d, step, g, val):
            fresh[way, d - 1, g] = val.astype(BF16)
            c = pltpu.make_async_remote_copy(
                src_ref=fresh.at[way, d - 1, g], dst_ref=land.at[way, d - 1, g],
                send_sem=send1.at[way, d - 1, g], recv_sem=recv1.at[way, d - 1, g],
                device_id=at(step if way == 0 else n - step), device_id_type=MESH)
            c.start()
            hops[way, d, g] = c
            pend.append(c)

        def got(way, d, g):
            hops[way, d, g].wait_recv()
            return land[way, d - 1, g].astype(F32)

        def chunk(d):
            project(0, (p + d) % n, rows)
            project(1, (p + n - d) % n, rows)

        def leaf(d):
            chunk(d)
            for i in range(G):
                for way in range(2):
                    g = i if way == 0 else G - 1 - i
                    send(way, d, 1, g, proj[way, :rows, lanes(g)])

        def inner(d, sources, step):
            chunk(d)
            for i in range(G):
                for way in range(2):
                    g = i if way == 0 else G - 1 - i
                    val = proj[way, :rows, lanes(g)]
                    for far in sources:
                        if far < n // 2 or near(way, g):
                            val = val + got(way, far, g)
                    send(way, d, step, g, val)

        project(0, (p + n // 2) % n, rows)
        for g in (0, G - 1) + tuple(range(1, G - 1)):
            send(0 if near(0, g) else 1, n // 2, 2, g, proj[0, :rows, lanes(g)])
        for at_step, (d, sources, step) in enumerate(plan):
            if at_step == 1:
                moments()
            if sources:
                inner(d, sources, step)
            else:
                leaf(d)
        project(0, p, rows)
        for g in range(G):
            val = proj[0, :rows, lanes(g)]
            for way in range(2):
                val = val + got(way, 1, g)
            stacked(g, val, n2)
        return pend

    def stacked(g, val, n2):
        for j in range(n2):
            sumf[j * PACK + g * BLK:j * PACK + (g + 1) * BLK, :] = val[j * BLK:(j + 1) * BLK, :]

    def direct_sum(n2, p2, at2, pend):
        msg[:n2] = sumf[:n2 * PACK, :].reshape(n2, PACK, LANES).astype(BF16)
        direct = []
        for k in far_first(n2):
            j = (p2 + k) % n2
            c = pltpu.make_async_remote_copy(
                src_ref=msg.at[j], dst_ref=land.at[k], send_sem=send2.at[k], recv_sem=recv2.at[k],
                device_id=at2(k), device_id_type=MESH)
            c.start()
            direct.append(c)
        total = sumf[pl.ds(pl.multiple_of(p2 * PACK, PACK), PACK), :]
        for i, k in reversed(list(enumerate(far_first(n2)))):
            direct[i].wait_recv()
            total = total + land[k].astype(F32)
        stack[...] = total
        return pend + direct

    def adam():
        for g in range(G):
            cols = slice(g * LANES, (g + 1) * LANES)
            low = stack[g * BLK:(g + 1) * BLK, :] / math.sqrt(tokens)
            first = m_old[:, cols] + 0.1 * low
            second = v_old[:, cols] + 0.001 * low * low
            m_ref[:, cols] = first
            v_ref[:, cols] = second
            norm[g * BLK:(g + 1) * BLK, :] = first / 0.19 / (jnp.sqrt(second / 0.001999) + 1e-8)

    def gather(n, p, at):
        gat[p] = norm[...].astype(BF16)
        sends = []
        for k in far_first(n):
            c = pltpu.make_async_remote_copy(
                src_ref=gat.at[p], dst_ref=gat.at[p], send_sem=send3.at[k], recv_sem=recv3.at[k],
                device_id=at(k), device_id_type=MESH)
            c.start()
            sends.append(c)
        for k in far_first(n)[::-1]:
            pltpu.make_async_remote_copy(
                src_ref=gat.at[p], dst_ref=gat.at[(p + n - k) % n], send_sem=send3.at[k], recv_sem=recv3.at[k],
                device_id=at(k), device_id_type=MESH).wait_recv()
        for b in range(n):
            part = gat[b].astype(F32)
            for g in range(G):
                rowsf[b * BLK:(b + 1) * BLK, g * LANES:(g + 1) * LANES] = part[g * BLK:(g + 1) * BLK, :]
        return sends

    def exchange(n, p, at, src, dst):
        sends = []
        for k in far_first(n):
            c = pltpu.make_async_remote_copy(
                src_ref=src.at[(p + k) % n], dst_ref=dst.at[p], send_sem=send4.at[k], recv_sem=recv4.at[k],
                device_id=at(k), device_id_type=MESH)
            c.start()
            sends.append(c)
        dst[p] = src[p]
        for k in far_first(n)[::-1]:
            pltpu.make_async_remote_copy(
                src_ref=src.at[p], dst_ref=dst.at[(p + n - k) % n], send_sem=send4.at[k], recv_sem=recv4.at[k],
                device_id=at(k), device_id_type=MESH).wait_recv()
        return sends

    nt = (((1,), (1,)), ((), ()))

    @pl.when(core == 0)
    def _():
        sends = direct_sum(NZ, z, at_z, tree_sum(
            NY, y, at_y, fresh_y, land_y, NZ * BLK, NZ, ((3, (), 1), (2, (3, 4), 1), (1, (2,), 1))))
        adam()
        sends += gather(NZ, z, at_z)
        for c in late:
            c.wait()
        prod = lax.dot_general(bsel[:NY * COLS, :], rowsf[...].astype(BF16), nt, preferred_element_type=F32)
        for yy in range(NY):
            wsend_y[yy] = prod[yy * COLS:(yy + 1) * COLS, :].astype(BF16)
        sends += exchange(NY, y, at_y, wsend_y, wland_y)
        w_ref[...] = jnp.concatenate([wland_y[yy] for yy in range(NY)], axis=1)
        for c in sends:
            c.wait_send()

    @pl.when(core == 1)
    def _():
        sends = direct_sum(NY, y, at_y, tree_sum(
            NZ, z, at_z, fresh_z, land_z, NY * BLK, NY,
            ((5, (), 1), (3, (), 1), (4, (5, 6), 2), (2, (3, 4), 1), (1, (2,), 1))))
        adam()
        sends += gather(NY, y, at_y)
        late_z.wait()
        part = NY // 2 * BLK
        rows = rowsf[:NY * BLK, :].astype(BF16)
        left = lax.broadcasted_iota(jnp.int32, (part, LANES), 1) < COLS
        for q in range(NZ // 2):
            pair = lax.dot_general(rows, bsel[q * LANES:(q + 1) * LANES, :], nt, preferred_element_type=F32)
            low, high = pair[:part, :], pair[part:, :]
            wsend_z[2 * q] = jnp.where(left, low, pltpu.roll(high, COLS, 1)).astype(BF16)
            wsend_z[2 * q + 1] = jnp.where(left, pltpu.roll(low, COLS, 1), high).astype(BF16)
        sends += exchange(NZ, z, at_z, wsend_z, wland_z)
        for zz in range(NZ):
            got = wland_z[zz].astype(F32)
            for b in range(NY // 2):
                at = b * NZ * BLK + zz * BLK
                wide[at:at + BLK, :] = got[b * BLK:(b + 1) * BLK, :]
        wt = wide[...].T.astype(BF16)
        w_ref[...] = jnp.concatenate([wt[:COLS, :], wt[COLS:, :]], axis=1)
        for c in sends:
            c.wait_send()

    for c in swaps:
        c.wait_send()


def store(wt, first_new, second_new, wt_out, first_out, second_out, sem):
    pairs = ((wt, wt_out), (first_new, first_out), (second_new, second_out))
    copies = [pltpu.make_async_copy(a, b, sem.at[i]) for i, (a, b) in enumerate(pairs)]
    for c in copies:
        c.start()
    for c in copies:
        c.wait()


def per_device(hidden_acts, out_grad, basis, code_first, scale_first, code_second, scale_second):
    tok, ff = hidden_acts.shape
    width = out_grad.shape[1]
    tokens = tok * lax.axis_size("dp")
    vm = pltpu.VMEM
    dma = pltpu.SemaphoreType.DMA
    any_spec = pl.BlockSpec(memory_space=pl.ANY)
    vmem_spec = pl.BlockSpec(memory_space=pltpu.VMEM)
    wt, first_new, second_new = pl.pallas_call(
        functools.partial(kernel, tokens=tokens),
        out_shape=(
            jax.ShapeDtypeStruct((COLS, ff), BF16),
            jax.ShapeDtypeStruct((BLK, RANK), F32),
            jax.ShapeDtypeStruct((BLK, RANK), F32),
        ),
        in_specs=[any_spec] * 7,
        out_specs=(vmem_spec,) * 3,
        scratch_shapes=[
            vm((tok, ff), BF16), vm((KC, tok, width // 2 // KC), BF16), vm((width // 2, RANK), BF16),
            vm((BLK, RANK), jnp.int32), vm((2, BLK), F32), vm((BLK, RANK), jnp.int32), vm((2, BLK), F32),
            vm((ff, tok), F32), vm((NY * BLK, tok), F32), vm((ff, tok), BF16),
            vm((2, tok, RANK // 2), F32), vm((2, tok, RANK // 2), F32), vm((tok, RANK), BF16), vm((2, NZ * BLK, RANK), F32),
            vm((BLK, RANK), F32), vm((BLK, RANK), F32),
            vm((2, NY // 2, G, NZ * BLK, LANES), BF16), vm((2, NZ // 2, G, NY * BLK, LANES), BF16),
            vm((2, NY // 2, G, NZ * BLK, LANES), BF16), vm((2, NZ // 2, G, NY * BLK, LANES), BF16),
            vm((NZ * PACK, LANES), F32), vm((NZ, PACK, LANES), BF16), vm((NZ, PACK, LANES), BF16),
            vm((PACK, LANES), F32), vm((PACK, LANES), F32), vm((NZ, PACK, LANES), BF16),
            vm((NZ * BLK, RANK), F32), vm((NZ * COLS, RANK), BF16),
            vm((NY, COLS, NZ * BLK), BF16), vm((NY, COLS, NZ * BLK), BF16),
            vm((NZ, PACK, LANES), BF16), vm((NZ, PACK, LANES), BF16), vm((ff // 2, LANES), F32),
            dma((2 * KC + 5 + NY,)), dma((2,)), dma((2,)), dma((2, NZ // 2, G)), dma((2, NZ // 2, G)),
            dma((NZ,)), dma((NZ,)), dma((NZ,)), dma((NZ,)), dma((NZ,)), dma((NZ,)),
        ],
        compiler_params=pltpu.CompilerParams(
            collective_id=0, has_side_effects=True, vmem_limit_bytes=44 * 1024 * 1024),
    )(*[pltpu.with_memory_space_constraint(a, pltpu.HBM) for a in (hidden_acts, out_grad, basis, code_first, scale_first.T, code_second, scale_second.T)])
    wt, first_new, second_new = pl.pallas_call(
        store,
        out_shape=[jax.ShapeDtypeStruct(a.shape, a.dtype) for a in (wt, first_new, second_new)],
        in_specs=[any_spec] * 3,
        out_specs=[any_spec] * 3,
        scratch_shapes=[dma((3,))],
        compiler_params=pltpu.CompilerParams(vmem_limit_bytes=1024 * 1024),
    )(wt, first_new, second_new)
    return wt.T, first_new, second_new


def solution(mesh):
    state = P(("mp", "dp"), None)
    return jax.shard_map(
        per_device,
        mesh=mesh,
        in_specs=(P("dp", "mp"), P("dp", None), P(), state, state, state, state),
        out_specs=(P("mp", "dp"), state, state),
        check_vma=False,
    )
```
